32 devices in a mesh: dp: 8 (over z, x), tensor: 4 (over y, core).
Axes of the slice: x: 2, y: 2, z: 4, core: 2. Of those that a mesh axis runs over, the one named last changes fastest.
Arguments:
- tokens: bfloat16 [16384, 768], P(('dp', 'tensor')), may hold values from -6 to 6
- ln1_gain: float32 [768], replicated, may hold values from 0.5 to 1.5
- ln1_shift: float32 [768], replicated, may hold values from -2 to 2
- qkv_weight: bfloat16 [3, 768, 768], P(None, None, 'tensor'), may hold values from -0.21875 to 0.21875
- qv_bias: float32 [2, 768], P(None, 'tensor'), may hold values from -2 to 2
- out_weight: bfloat16 [768, 768], P('tensor'), may hold values from -1.75 to 1.75
- out_bias: float32 [768], replicated, may hold values from -2 to 2
- ln2_gain: float32 [768], replicated, may hold values from 0.5 to 1.5
- ln2_shift: float32 [768], replicated, may hold values from -2 to 2
- fc_weight: bfloat16 [768, 3072], P(None, 'tensor'), may hold values from -0.21875 to 0.21875
- fc_bias: float32 [3072], P('tensor'), may hold values from -2 to 2
- proj_weight: bfloat16 [3072, 768], P('tensor'), may hold values from -0.109375 to 0.109375
- proj_bias: float32 [768], replicated, may hold values from -2 to 2
- cotangent: bfloat16 [16384, 768], P(('dp', 'tensor')), may hold values from -6 to 6
Outputs:
- output: bfloat16 [16384, 768], P(('dp', 'tensor'))
- tokens_grad: float32 [16384, 768], P(('dp', 'tensor'))
- ln1_gain_grad: float32 [768], replicated
- ln1_shift_grad: float32 [768], replicated
- qkv_weight_grad: float32 [3, 768, 768], P(None, None, 'tensor')
- qv_bias_grad: float32 [2, 768], P(None, 'tensor')
- out_weight_grad: float32 [768, 768], P('tensor')
- out_bias_grad: float32 [768], replicated
- ln2_gain_grad: float32 [768], replicated
- ln2_shift_grad: float32 [768], replicated
- fc_weight_grad: float32 [768, 3072], P(None, 'tensor')
- fc_bias_grad: float32 [3072], P('tensor')
- proj_weight_grad: float32 [3072, 768], P('tensor')
- proj_bias_grad: float32 [768], replicated
The draws below stay inside these ranges and needn't reach their ends.
All inputs are finite; a program needn't handle non-finite values.
Results may differ from the reference program's by a relative error of at most 0.018.
Values may be sent and summed in bfloat16 or wider, within the bound.
A program may use at most 128 MiB of HBM per device.

```python
import jax
import jax.numpy as jnp
from jax import lax

D = 768
HEADS = 12
HEAD_DIM = 64
FF = 3072
LEN = 1024
TOKENS = 16384


def levels(key, dims, shards, least, top_value):
    level = 1.0
    for axis_at, shards_of in shards:
        steps = jax.random.uniform(jax.random.fold_in(jax.random.fold_in(key, 6), axis_at), (shards_of,), jnp.float32, least / len(shards), top_value / len(shards))
        level = level * jnp.repeat(jnp.exp(steps), dims[axis_at] // shards_of).reshape((-1,) + (1,) * (len(dims) - 1 - axis_at))
    return level


def normal_values(stream_key, extent, deviation, limit, shards=(), kind=jnp.bfloat16):
    entries = jax.random.normal(stream_key, extent, jnp.float32) * deviation
    if len(shards) > 0:
        entries = levels(stream_key, extent, shards, -0.22, 0.18) * entries
    return jnp.clip(entries, min=-limit, max=limit).astype(kind)


def setup_inputs(seed: int = 0) -> dict:
    keys = jax.random.split(jax.random.key(seed), 15)
    tokens = normal_values(keys[0], (TOKENS, D), 1.0, 6.0, ((0, 32),))
    ln1_gain = jnp.clip(1.0 + 0.1 * jax.random.normal(keys[1], (D,), jnp.float32), 0.5, 1.5)
    ln1_shift = normal_values(keys[2], (D,), 0.3, 2.0, (), jnp.float32)
    qkv_weight = normal_values(keys[3], (3, D, D), D ** -0.5, 0.21875, ((2, 4),))
    qv_bias = normal_values(keys[4], (2, D), 0.3, 2.0, ((1, 4),), jnp.float32)
    out_weight = normal_values(keys[5], (D, D), (D // 64) ** -0.5, 1.75, ((0, 4),))
    out_bias = normal_values(keys[6], (D,), 0.3, 2.0, (), jnp.float32)
    ln2_gain = jnp.clip(1.0 + 0.1 * jax.random.normal(keys[7], (D,), jnp.float32), 0.5, 1.5)
    ln2_shift = normal_values(keys[8], (D,), 0.3, 2.0, (), jnp.float32)
    fc_weight = normal_values(keys[9], (D, FF), D ** -0.5, 0.21875, ((1, 4),))
    fc_bias = normal_values(keys[10], (FF,), 0.3, 2.0, ((0, 4),), jnp.float32)
    proj_weight = normal_values(keys[11], (FF, D), FF ** -0.5, 0.109375, ((0, 4),))
    proj_bias = normal_values(keys[12], (D,), 0.3, 2.0, (), jnp.float32)
    cotangent = normal_values(keys[13], (TOKENS, D), 1.0, 6.0, ((0, 32),))
    return dict(tokens=tokens, ln1_gain=ln1_gain, ln1_shift=ln1_shift, qkv_weight=qkv_weight, qv_bias=qv_bias, out_weight=out_weight, out_bias=out_bias, ln2_gain=ln2_gain, ln2_shift=ln2_shift, fc_weight=fc_weight, fc_bias=fc_bias, proj_weight=proj_weight, proj_bias=proj_bias, cotangent=cotangent)


NORM_EPSILON = 1e-05
HIGHEST = lax.Precision.HIGHEST

@jax.custom_vjp
def low(v):
    return lax.optimization_barrier(v.astype(jnp.bfloat16)).astype(jnp.float32)

@jax.custom_vjp
def low_back(v):
    return v

def low_keep(v):
    return (low(v), None)

def low_pass(kept, grad):
    return (grad,)

def back_keep(v):
    return (v, None)

def back_low(kept, grad):
    return (low(grad),)
low.defvjp(low_keep, low_pass)
low_back.defvjp(back_keep, back_low)

def layer_norm(values, gain_vec, shift_vec):
    row_mean = lax.optimization_barrier(jnp.mean(values, axis=-1, keepdims=True))
    centred = values - row_mean
    variance = lax.optimization_barrier(jnp.mean(centred * centred, axis=-1, keepdims=True))
    return centred * lax.rsqrt(variance + NORM_EPSILON) * gain_vec + shift_vec

def matmul(left, right):
    return jnp.dot(left, right, precision=HIGHEST, preferred_element_type=jnp.float32)

def attend(seq_block):
    query, key_rows, value_rows = (seq_block[0], seq_block[1], seq_block[2])
    length = query.shape[1]
    raw_scores = jnp.einsum('hqd,hkd->hqk', query, key_rows, precision=HIGHEST) * HEAD_DIM ** (-0.5)
    scores = low_back(raw_scores)
    causal = lax.broadcasted_iota(jnp.int32, (length, length), 0) >= lax.broadcasted_iota(jnp.int32, (length, length), 1)
    masked = jnp.where(causal[None], scores, -1e+30)
    row_max = lax.optimization_barrier(jnp.max(masked, axis=-1, keepdims=True))
    exponent = jnp.exp(masked - row_max)
    row_total = lax.optimization_barrier(jnp.sum(exponent, axis=-1, keepdims=True))
    weights = low(exponent / row_total)
    return jnp.einsum('hqk,hkd->hqd', weights, value_rows, precision=HIGHEST)

def forward(tok_rows, ln1_gain, ln1_shift, qkv_weight, qv_bias, out_weight, out_bias, ln2_gain, ln2_shift, fc_weight, fc_bias, proj_weight, proj_bias):
    first = low(layer_norm(tok_rows, ln1_gain, ln1_shift))
    qkv_flat = jnp.transpose(qkv_weight, (1, 0, 2)).reshape(D, 3 * D)
    qkv_shift = jnp.concatenate([qv_bias[0], jnp.zeros_like(qv_bias[0]), qv_bias[1]])
    qkv_all = low(low_back(matmul(first, qkv_flat) + qkv_shift))
    seq_blocks = qkv_all.reshape(-1, LEN, 3, HEADS, HEAD_DIM).transpose(0, 2, 3, 1, 4)
    attended = lax.map(jax.checkpoint(attend), seq_blocks)
    heads_out = low(low_back(attended.transpose(0, 2, 1, 3).reshape(-1, D)))
    branch = low_back(matmul(heads_out, out_weight) + out_bias)
    resid = tok_rows + branch
    second = low(layer_norm(resid, ln2_gain, ln2_shift))
    hidden = low_back(matmul(second, fc_weight) + fc_bias)
    active = low(jax.nn.gelu(hidden, approximate=True))
    return resid + matmul(active, proj_weight) + proj_bias

def reference(tokens, ln1_gain, ln1_shift, qkv_weight, qv_bias, out_weight, out_bias, ln2_gain, ln2_shift, fc_weight, fc_bias, proj_weight, proj_bias, cotangent):
    inputs = (tokens, ln1_gain, ln1_shift, qkv_weight, qv_bias, out_weight, out_bias, ln2_gain, ln2_shift, fc_weight, fc_bias, proj_weight, proj_bias)
    inputs = tuple((item.astype(jnp.float32) for item in inputs))
    result, backward = jax.vjp(forward, *inputs)
    grads = backward(cotangent.astype(jnp.float32))
    return (result.astype(jnp.bfloat16), grads[0], grads[1], grads[2], grads[3], grads[4], grads[5], grads[6], grads[7], grads[8], grads[9], grads[10], grads[11], grads[12])
```

```python
from functools import partial

import jax
import jax.numpy as jnp
from jax import lax
from jax.experimental import pallas as pl
from jax.experimental.pallas import tpu as pltpu
from jax.sharding import PartitionSpec as P

HEAD_DIM = 64
PAIR = 2 * HEAD_DIM
LEN = 1024
BLOCK = 256
NORM_EPSILON = 1e-05
SCORE_SCALE = 1.4426950408889634 * HEAD_DIM**-0.5

ROWS_ROWS = (((1,), (1,)), ((), ()))


def normalize(values):
    row_mean = jnp.mean(values, axis=-1, keepdims=True)
    centred = values - row_mean
    variance = jnp.mean(centred * centred, axis=-1, keepdims=True)
    row_scale = lax.rsqrt(variance + NORM_EPSILON)
    return (centred * row_scale, row_scale)


def norm_back(grad_in, normed, row_scale, gain_vec):
    shaped = grad_in * gain_vec
    return row_scale * (
        shaped
        - jnp.mean(shaped, axis=-1, keepdims=True)
        - normed * jnp.mean(shaped * normed, axis=-1, keepdims=True)
    )


def dot32(left, right, dims=(((1,), (0,)), ((), ()))):
    return lax.dot_general(left, right, dims, preferred_element_type=jnp.float32)


def half_starts(core_ref):
    half = LEN // 2
    first = pl.multiple_of(core_ref[0] * half, half)
    second = pl.multiple_of(half - core_ref[0] * half, half)
    return first, second


def in_order(ref, starts):
    half = LEN // 2
    return jnp.concatenate([ref[pl.ds(start, half), :] for start in starts], axis=0)


def block_rows(starts, step):
    half = LEN // 2
    offset = step * BLOCK
    start = starts[offset // half] + offset % half
    return pl.ds(pl.multiple_of(start, BLOCK), BLOCK)


def split_heads(block):
    low_lanes = lax.broadcasted_iota(jnp.int32, block.shape, 1) < HEAD_DIM
    zero = jnp.zeros_like(block)
    return jnp.concatenate(
        [jnp.where(low_lanes, block, zero), jnp.where(low_lanes, zero, block)], axis=0
    )


def causal_keep():
    keys = lax.broadcasted_iota(jnp.int32, (BLOCK, 2 * BLOCK), 0)
    queries = lax.broadcasted_iota(jnp.int32, (BLOCK, 2 * BLOCK), 1) % BLOCK
    return keys <= queries


def attend_forward_kernel(core_ref, qkv_ref, out_ref, log_ref):
    starts = half_starts(core_ref)
    full = in_order(qkv_ref, starts)
    keys = full[:, PAIR : 2 * PAIR]
    values_t = full[:, 2 * PAIR :].T
    keep = causal_keep()
    for step in range(LEN // BLOCK):
        seen = (step + 1) * BLOCK
        queries = split_heads(full[step * BLOCK : seen, :PAIR])
        scores = dot32(keys[:seen], queries, ROWS_ROWS)
        last = jnp.where(keep, scores[seen - BLOCK :], -1e30)
        scores = jnp.concatenate([scores[: seen - BLOCK], last], axis=0) if step else last
        top = jnp.max(scores, axis=0, keepdims=True) * SCORE_SCALE
        exponent = jnp.exp2(scores * SCORE_SCALE - top)
        total = jnp.sum(exponent, axis=0, keepdims=True)
        low = exponent.astype(jnp.bfloat16)
        inverse = 1.0 / total
        logs = top + jnp.log2(total)
        parts = []
        for head in range(2):
            columns = slice(head * BLOCK, (head + 1) * BLOCK)
            attended = dot32(
                values_t[head * HEAD_DIM : (head + 1) * HEAD_DIM, :seen], low[:, columns]
            )
            parts.append(attended * inverse[:, columns])
            log_ref[0, head : head + 1, step * BLOCK : seen] = logs[:, columns]
        out_ref[block_rows(starts, step), :] = (
            jnp.concatenate(parts, axis=0).T.astype(jnp.bfloat16)
        )


def attend_backward_kernel(core_ref, qkv_ref, out_ref, log_ref, grad_ref, dqkv_ref, dk_ref, dv_ref):
    starts = half_starts(core_ref)
    full = in_order(qkv_ref, starts)
    out_grad = in_order(grad_ref, starts)
    attended = in_order(out_ref, starts)
    keys = full[:, PAIR : 2 * PAIR]
    values = full[:, 2 * PAIR :]
    keys_t = keys.T
    product_t = (out_grad.astype(jnp.float32) * attended.astype(jnp.float32)).T
    deltas = [
        jnp.sum(product_t[head * HEAD_DIM : (head + 1) * HEAD_DIM], axis=0, keepdims=True)
        for head in range(2)
    ]
    keep = causal_keep()
    factor = HEAD_DIM**-0.5
    steps = LEN // BLOCK
    for step in reversed(range(steps)):
        seen = (step + 1) * BLOCK
        columns = slice(step * BLOCK, seen)
        queries = split_heads(full[columns, :PAIR])
        grads = split_heads(out_grad[columns])
        logs = jnp.concatenate([log_ref[0, 0:1, columns], log_ref[0, 1:2, columns]], axis=1)
        delta = jnp.concatenate([deltas[0][:, columns], deltas[1][:, columns]], axis=1)
        scores = dot32(keys[:seen], queries, ROWS_ROWS)
        weights = jnp.exp2(scores * SCORE_SCALE - logs)
        last = jnp.where(keep, weights[seen - BLOCK :], 0.0)
        weights = jnp.concatenate([weights[: seen - BLOCK], last], axis=0) if step else last
        weight_grad = dot32(values[:seen], grads, ROWS_ROWS)
        value_term = dot32(weights.astype(jnp.bfloat16), grads)
        score_grad = (weights * (weight_grad - delta)).astype(jnp.bfloat16)
        key_term = dot32(score_grad, queries)
        if step == steps - 1:
            dk_ref[...] = key_term
            dv_ref[...] = value_term
        else:
            dk_ref[:seen, :] += key_term
            dv_ref[:seen, :] += value_term
        parts = [
            dot32(
                keys_t[head * HEAD_DIM : (head + 1) * HEAD_DIM, :seen],
                score_grad[:, head * BLOCK : (head + 1) * BLOCK],
            )
            for head in range(2)
        ]
        query_grad = jnp.concatenate(parts, axis=0).T * factor
        dqkv_ref[block_rows(starts, step), :PAIR] = query_grad.astype(jnp.bfloat16)
    half = LEN // 2
    for at, start in enumerate(starts):
        rows = slice(at * half, (at + 1) * half)
        dqkv_ref[pl.ds(start, half), PAIR : 2 * PAIR] = (dk_ref[rows, :] * factor).astype(
            jnp.bfloat16
        )
        dqkv_ref[pl.ds(start, half), 2 * PAIR :] = dv_ref[rows, :].astype(jnp.bfloat16)


def pair_block(width):
    return pl.BlockSpec((LEN, width), lambda pair, core: (0, pair))


LOG_BLOCK = pl.BlockSpec((1, 8, LEN), lambda pair, core: (pair, 0, 0))
KERNEL_PARAMS = pltpu.CompilerParams(vmem_limit_bytes=40 * 1024 * 1024)


def attend_forward(core, qkv):
    pairs = qkv.shape[1] // (3 * PAIR)
    return pl.pallas_call(
        attend_forward_kernel,
        grid_spec=pltpu.PrefetchScalarGridSpec(
            num_scalar_prefetch=1,
            grid=(pairs,),
            in_specs=[pair_block(3 * PAIR)],
            out_specs=[pair_block(PAIR), LOG_BLOCK],
        ),
        out_shape=[
            jax.ShapeDtypeStruct((LEN, pairs * PAIR), jnp.bfloat16),
            jax.ShapeDtypeStruct((pairs, 8, LEN), jnp.float32),
        ],
        compiler_params=KERNEL_PARAMS,
        cost_estimate=pl.CostEstimate(
            flops=pairs * 5 * LEN * LEN * PAIR,
            bytes_accessed=pairs * LEN * PAIR * 8,
            transcendentals=pairs * LEN * LEN,
        ),
        name="attend_forward",
    )(core, qkv)


def attend_backward(core, qkv, attended, logs, out_grad):
    pairs = qkv.shape[1] // (3 * PAIR)
    return pl.pallas_call(
        attend_backward_kernel,
        grid_spec=pltpu.PrefetchScalarGridSpec(
            num_scalar_prefetch=1,
            grid=(pairs,),
            in_specs=[pair_block(3 * PAIR), pair_block(PAIR), LOG_BLOCK, pair_block(PAIR)],
            out_specs=pair_block(3 * PAIR),
            scratch_shapes=[
                pltpu.VMEM((LEN, PAIR), jnp.float32),
                pltpu.VMEM((LEN, PAIR), jnp.float32),
            ],
        ),
        out_shape=jax.ShapeDtypeStruct(qkv.shape, jnp.bfloat16),
        compiler_params=KERNEL_PARAMS,
        cost_estimate=pl.CostEstimate(
            flops=pairs * 14 * LEN * LEN * PAIR,
            bytes_accessed=pairs * LEN * PAIR * 16,
            transcendentals=pairs * LEN * LEN,
        ),
        name="attend_backward",
    )(core, qkv, attended, logs, out_grad)


def local(
    tokens,
    ln1_gain,
    ln1_shift,
    qkv_weight,
    qv_bias,
    out_weight,
    out_bias,
    ln2_gain,
    ln2_shift,
    fc_weight,
    fc_bias,
    proj_weight,
    proj_bias,
    cotangent,
):
    size = lax.axis_size("tensor")
    place = lax.axis_index("tensor")
    near = [(i, i ^ 1) for i in range(size)]
    far = [(i, (i + size // 2) % size) for i in range(size)]
    core = (place % 2).astype(jnp.int32).reshape(1)
    own_rows, d = tokens.shape
    width = qkv_weight.shape[2]
    hidden_width = fc_weight.shape[1]
    assert size == 4 and 2 * own_rows == LEN

    def from_near(value):
        return lax.ppermute(value, "tensor", near)

    def from_far(value):
        return lax.ppermute(value, "tensor", far)

    biases = jnp.concatenate([qv_bias.reshape(-1), fc_bias])
    far_biases = from_far(biases)
    far_qkv = from_far(qkv_weight)
    far_out = from_far(out_weight)
    far_fc = from_far(fc_weight)
    far_proj = from_far(proj_weight)
    near_cotangent = from_near(cotangent)

    tok_rows = tokens.astype(jnp.float32)
    normed1, scale1 = normalize(tok_rows)
    first_own = (normed1 * ln1_gain + ln1_shift).astype(jnp.bfloat16)
    first = jnp.concatenate([first_own, from_near(first_own)], axis=0)

    pairs = 2 * width // PAIR
    qkv_both = jnp.concatenate([qkv_weight, far_qkv], axis=2)
    qkv_flat = qkv_both.reshape(3, d, pairs, PAIR).transpose(1, 2, 0, 3).reshape(d, -1)
    far_qv = far_biases[: 2 * width].reshape(2, width)
    qv_both = jnp.concatenate([qv_bias, far_qv], axis=1).reshape(2, pairs, PAIR)
    qkv_shift = jnp.stack([qv_both[0], jnp.zeros_like(qv_both[0]), qv_both[1]], axis=1).reshape(-1)
    qkv = (dot32(first, qkv_flat) + qkv_shift).astype(jnp.bfloat16)
    attended, logs = attend_forward(core, qkv)

    out_both = jnp.concatenate([out_weight, far_out], axis=0)
    branch_far = from_near(dot32(attended[own_rows:], out_both).astype(jnp.bfloat16))
    branch = dot32(attended[:own_rows], out_both) + branch_far.astype(jnp.float32)
    resid = tok_rows + branch + out_bias
    normed2, scale2 = normalize(resid)
    second_own = (normed2 * ln2_gain + ln2_shift).astype(jnp.bfloat16)
    second = jnp.concatenate([second_own, from_near(second_own)], axis=0)

    fc_both = jnp.concatenate([fc_weight, far_fc], axis=1)
    fc_shift = jnp.concatenate([fc_bias, far_biases[2 * width :]])
    proj_both = jnp.concatenate([proj_weight, far_proj], axis=0)
    hidden = dot32(second, fc_both) + fc_shift
    active, gelu_back = jax.vjp(partial(jax.nn.gelu, approximate=True), hidden)
    active_low = active.astype(jnp.bfloat16)
    mlp_far = from_near(dot32(active_low[own_rows:], proj_both).astype(jnp.bfloat16))
    mlp_out = dot32(active_low[:own_rows], proj_both) + mlp_far.astype(jnp.float32)
    output = (resid + mlp_out + proj_bias).astype(jnp.bfloat16)

    grad_rows = cotangent.astype(jnp.float32)
    proj_bias_grad = jnp.sum(grad_rows, axis=0)
    grad_full = jnp.concatenate([cotangent, near_cotangent], axis=0)
    active_grad = dot32(grad_full, proj_both, ROWS_ROWS)
    hidden_low = gelu_back(active_grad)[0].astype(jnp.bfloat16)
    second_far = from_near(
        dot32(hidden_low[own_rows:], fc_both, ROWS_ROWS).astype(jnp.bfloat16)
    )
    second_grad = dot32(hidden_low[:own_rows], fc_both, ROWS_ROWS) + second_far.astype(jnp.float32)

    columns_columns = (((0,), (0,)), ((), ()))

    def summed(own, other):
        return lax.psum((own + other.astype(jnp.float32)).astype(jnp.bfloat16), "dp").astype(
            jnp.float32
        )

    proj_far = from_far(
        dot32(active_low[:, hidden_width:], grad_full, columns_columns).astype(jnp.bfloat16)
    )
    proj_own = dot32(active_low[:, :hidden_width], grad_full, columns_columns)
    proj_weight_grad = summed(proj_own, proj_far)
    fc_far = from_far(
        dot32(second, hidden_low[:, hidden_width:], columns_columns).astype(jnp.bfloat16)
    )
    fc_own = dot32(second, hidden_low[:, :hidden_width], columns_columns)
    fc_weight_grad = summed(fc_own, fc_far)
    fc_sums = jnp.sum(hidden_low, axis=0, dtype=jnp.float32)

    resid_grad = grad_rows + norm_back(second_grad, normed2, scale2, ln2_gain)
    branch_low = resid_grad.astype(jnp.bfloat16)
    branch_full = jnp.concatenate([branch_low, from_near(branch_low)], axis=0)
    ln2_gain_grad = jnp.sum(second_grad * normed2, axis=0)
    ln2_shift_grad = jnp.sum(second_grad, axis=0)
    out_bias_grad = jnp.sum(branch_low, axis=0, dtype=jnp.float32)
    heads_grad = dot32(branch_full, out_both, ROWS_ROWS).astype(jnp.bfloat16)
    out_far = from_far(
        dot32(attended[:, width:], branch_full, columns_columns).astype(jnp.bfloat16)
    )
    out_own = dot32(attended[:, :width], branch_full, columns_columns)
    out_weight_grad = summed(out_own, out_far)

    qkv_grad = attend_backward(core, qkv, attended, logs, heads_grad)
    qkv_sums = jnp.sum(qkv_grad, axis=0, dtype=jnp.float32).reshape(pairs, 3, PAIR)
    qv_sums = qkv_sums[:, 0::2].transpose(1, 0, 2).reshape(2, 2 * width)
    qkv_both_grad = dot32(first, qkv_grad, columns_columns)
    qkv_both_grad = qkv_both_grad.reshape(d, pairs, 3, PAIR).transpose(2, 0, 1, 3)
    qkv_both_grad = qkv_both_grad.reshape(3, d, 2 * width)
    qkv_far = from_far(qkv_both_grad[:, :, width:].astype(jnp.bfloat16))
    qkv_weight_grad = summed(qkv_both_grad[:, :, :width], qkv_far)

    first_far = from_near(dot32(qkv_grad[own_rows:], qkv_flat, ROWS_ROWS).astype(jnp.bfloat16))
    first_grad = dot32(qkv_grad[:own_rows], qkv_flat, ROWS_ROWS) + first_far.astype(jnp.float32)
    ln1_gain_grad = jnp.sum(first_grad * normed1, axis=0)
    ln1_shift_grad = jnp.sum(first_grad, axis=0)
    tokens_grad = resid_grad + norm_back(first_grad, normed1, scale1, ln1_gain)

    other = (place + size // 2) % size
    split = jnp.zeros((size, 2 * width + hidden_width), jnp.float32)
    for at, columns in ((place, slice(0, 1)), (other, slice(1, 2))):
        part = jnp.concatenate(
            [
                qv_sums.reshape(2, 2, width)[:, columns].reshape(-1),
                fc_sums.reshape(2, hidden_width)[columns].reshape(-1),
            ]
        )
        split = lax.dynamic_update_slice(split, part[None], (at, 0))
    whole = jnp.concatenate(
        [
            ln1_gain_grad,
            ln1_shift_grad,
            out_bias_grad,
            ln2_gain_grad,
            ln2_shift_grad,
            proj_bias_grad,
            split.reshape(-1),
        ]
    )
    whole = lax.psum(whole, ("dp", "tensor"))
    ln1_gain_grad, ln1_shift_grad, out_bias_grad, ln2_gain_grad, ln2_shift_grad, proj_bias_grad = (
        whole[at * d : (at + 1) * d] for at in range(6)
    )
    mine = lax.dynamic_index_in_dim(whole[6 * d :].reshape(size, -1), place, 0, keepdims=False)
    qv_bias_grad = mine[: 2 * width].reshape(2, width)
    fc_bias_grad = mine[2 * width :]
    return (
        output,
        tokens_grad,
        ln1_gain_grad,
        ln1_shift_grad,
        qkv_weight_grad,
        qv_bias_grad,
        out_weight_grad,
        out_bias_grad,
        ln2_gain_grad,
        ln2_shift_grad,
        fc_weight_grad,
        fc_bias_grad,
        proj_weight_grad,
        proj_bias_grad,
    )


def solution(mesh):
    return jax.shard_map(
        local,
        mesh=mesh,
        in_specs=(
            P(("dp", "tensor"), None),
            P(),
            P(),
            P(None, None, "tensor"),
            P(None, "tensor"),
            P("tensor", None),
            P(),
            P(),
            P(),
            P(None, "tensor"),
            P("tensor"),
            P("tensor", None),
            P(),
            P(("dp", "tensor"), None),
        ),
        out_specs=(
            P(("dp", "tensor"), None),
            P(("dp", "tensor"), None),
            P(),
            P(),
            P(None, None, "tensor"),
            P(None, "tensor"),
            P("tensor", None),
            P(),
            P(),
            P(),
            P(None, "tensor"),
            P("tensor"),
            P("tensor", None),
            P(),
        ),
        check_vma=False,
    )
```

```python
from functools import partial

import jax
import jax.numpy as jnp
from jax import lax
from jax.experimental import pallas as pl
from jax.experimental.pallas import tpu as pltpu
from jax.sharding import PartitionSpec as P

HEAD_DIM = 64
PAIR = 2 * HEAD_DIM
LEN = 1024
BLOCK = 256
NORM_EPSILON = 1e-05
SCORE_SCALE = 1.4426950408889634 * HEAD_DIM**-0.5

ROWS_ROWS = (((1,), (1,)), ((), ()))


def normalize(values):
    row_mean = jnp.mean(values, axis=-1, keepdims=True)
    centred = values - row_mean
    variance = jnp.mean(centred * centred, axis=-1, keepdims=True)
    row_scale = lax.rsqrt(variance + NORM_EPSILON)
    return (centred * row_scale, row_scale)


def norm_back(grad_in, normed, row_scale, gain_vec):
    shaped = grad_in * gain_vec
    return row_scale * (
        shaped
        - jnp.mean(shaped, axis=-1, keepdims=True)
        - normed * jnp.mean(shaped * normed, axis=-1, keepdims=True)
    )


def dot32(left, right, dims=(((1,), (0,)), ((), ()))):
    return lax.dot_general(left, right, dims, preferred_element_type=jnp.float32)


def half_starts(core_ref):
    half = LEN // 2
    first = pl.multiple_of(core_ref[0] * half, half)
    second = pl.multiple_of(half - core_ref[0] * half, half)
    return first, second


def in_order(ref, starts):
    half = LEN // 2
    return jnp.concatenate([ref[pl.ds(start, half), :] for start in starts], axis=0)


def block_rows(starts, step):
    half = LEN // 2
    offset = step * BLOCK
    start = starts[offset // half] + offset % half
    return pl.ds(pl.multiple_of(start, BLOCK), BLOCK)


def split_heads(block):
    low_lanes = lax.broadcasted_iota(jnp.int32, block.shape, 1) < HEAD_DIM
    zero = jnp.zeros_like(block)
    return jnp.concatenate(
        [jnp.where(low_lanes, block, zero), jnp.where(low_lanes, zero, block)], axis=0
    )


def causal_keep():
    keys = lax.broadcasted_iota(jnp.int32, (BLOCK, 2 * BLOCK), 0)
    queries = lax.broadcasted_iota(jnp.int32, (BLOCK, 2 * BLOCK), 1) % BLOCK
    return keys <= queries


def attend_forward_kernel(core_ref, qkv_ref, out_ref, log_ref):
    starts = half_starts(core_ref)
    full = in_order(qkv_ref, starts)
    keys = full[:, PAIR : 2 * PAIR]
    values_t = full[:, 2 * PAIR :].T
    keep = causal_keep()
    for step in range(LEN // BLOCK):
        seen = (step + 1) * BLOCK
        queries = split_heads(full[step * BLOCK : seen, :PAIR])
        scores = dot32(keys[:seen], queries, ROWS_ROWS)
        last = jnp.where(keep, scores[seen - BLOCK :], -1e30)
        scores = jnp.concatenate([scores[: seen - BLOCK], last], axis=0) if step else last
        top = jnp.max(scores, axis=0, keepdims=True) * SCORE_SCALE
        exponent = jnp.exp2(scores * SCORE_SCALE - top)
        total = jnp.sum(exponent, axis=0, keepdims=True)
        low = exponent.astype(jnp.bfloat16)
        inverse = 1.0 / total
        logs = top + jnp.log2(total)
        parts = []
        for head in range(2):
            columns = slice(head * BLOCK, (head + 1) * BLOCK)
            attended = dot32(
                values_t[head * HEAD_DIM : (head + 1) * HEAD_DIM, :seen], low[:, columns]
            )
            parts.append(attended * inverse[:, columns])
            log_ref[0, head : head + 1, step * BLOCK : seen] = logs[:, columns]
        out_ref[block_rows(starts, step), :] = (
            jnp.concatenate(parts, axis=0).T.astype(jnp.bfloat16)
        )


def attend_backward_kernel(core_ref, qkv_ref, out_ref, log_ref, grad_ref, dqkv_ref, dk_ref, dv_ref):
    starts = half_starts(core_ref)
    full = in_order(qkv_ref, starts)
    out_grad = in_order(grad_ref, starts)
    attended = in_order(out_ref, starts)
    keys = full[:, PAIR : 2 * PAIR]
    values = full[:, 2 * PAIR :]
    keys_t = keys.T
    product_t = (out_grad.astype(jnp.float32) * attended.astype(jnp.float32)).T
    deltas = [
        jnp.sum(product_t[head * HEAD_DIM : (head + 1) * HEAD_DIM], axis=0, keepdims=True)
        for head in range(2)
    ]
    keep = causal_keep()
    factor = HEAD_DIM**-0.5
    steps = LEN // BLOCK
    for step in reversed(range(steps)):
        seen = (step + 1) * BLOCK
        columns = slice(step * BLOCK, seen)
        queries = split_heads(full[columns, :PAIR])
        grads = split_heads(out_grad[columns])
        logs = jnp.concatenate([log_ref[0, 0:1, columns], log_ref[0, 1:2, columns]], axis=1)
        delta = jnp.concatenate([deltas[0][:, columns], deltas[1][:, columns]], axis=1)
        scores = dot32(keys[:seen], queries, ROWS_ROWS)
        weights = jnp.exp2(scores * SCORE_SCALE - logs)
        last = jnp.where(keep, weights[seen - BLOCK :], 0.0)
        weights = jnp.concatenate([weights[: seen - BLOCK], last], axis=0) if step else last
        weight_grad = dot32(values[:seen], grads, ROWS_ROWS)
        value_term = dot32(weights.astype(jnp.bfloat16), grads)
        score_grad = (weights * (weight_grad - delta)).astype(jnp.bfloat16)
        key_term = dot32(score_grad, queries)
        if step == steps - 1:
            dk_ref[...] = key_term
            dv_ref[...] = value_term
        else:
            dk_ref[:seen, :] += key_term
            dv_ref[:seen, :] += value_term
        parts = [
            dot32(
                keys_t[head * HEAD_DIM : (head + 1) * HEAD_DIM, :seen],
                score_grad[:, head * BLOCK : (head + 1) * BLOCK],
            )
            for head in range(2)
        ]
        query_grad = jnp.concatenate(parts, axis=0).T * factor
        dqkv_ref[block_rows(starts, step), :PAIR] = query_grad.astype(jnp.bfloat16)
    half = LEN // 2
    for at, start in enumerate(starts):
        rows = slice(at * half, (at + 1) * half)
        dqkv_ref[pl.ds(start, half), PAIR : 2 * PAIR] = (dk_ref[rows, :] * factor).astype(
            jnp.bfloat16
        )
        dqkv_ref[pl.ds(start, half), 2 * PAIR :] = dv_ref[rows, :].astype(jnp.bfloat16)


def pair_block(width):
    return pl.BlockSpec((LEN, width), lambda pair, core: (0, pair))


LOG_BLOCK = pl.BlockSpec((1, 8, LEN), lambda pair, core: (pair, 0, 0))
KERNEL_PARAMS = pltpu.CompilerParams(vmem_limit_bytes=40 * 1024 * 1024)


def attend_forward(core, qkv):
    pairs = qkv.shape[1] // (3 * PAIR)
    return pl.pallas_call(
        attend_forward_kernel,
        grid_spec=pltpu.PrefetchScalarGridSpec(
            num_scalar_prefetch=1,
            grid=(pairs,),
            in_specs=[pair_block(3 * PAIR)],
            out_specs=[pair_block(PAIR), LOG_BLOCK],
        ),
        out_shape=[
            jax.ShapeDtypeStruct((LEN, pairs * PAIR), jnp.bfloat16),
            jax.ShapeDtypeStruct((pairs, 8, LEN), jnp.float32),
        ],
        compiler_params=KERNEL_PARAMS,
        cost_estimate=pl.CostEstimate(
            flops=pairs * 5 * LEN * LEN * PAIR,
            bytes_accessed=pairs * LEN * PAIR * 8,
            transcendentals=pairs * LEN * LEN,
        ),
        name="attend_forward",
    )(core, qkv)


def attend_backward(core, qkv, attended, logs, out_grad):
    pairs = qkv.shape[1] // (3 * PAIR)
    return pl.pallas_call(
        attend_backward_kernel,
        grid_spec=pltpu.PrefetchScalarGridSpec(
            num_scalar_prefetch=1,
            grid=(pairs,),
            in_specs=[pair_block(3 * PAIR), pair_block(PAIR), LOG_BLOCK, pair_block(PAIR)],
            out_specs=pair_block(3 * PAIR),
            scratch_shapes=[
                pltpu.VMEM((LEN, PAIR), jnp.float32),
                pltpu.VMEM((LEN, PAIR), jnp.float32),
            ],
        ),
        out_shape=jax.ShapeDtypeStruct(qkv.shape, jnp.bfloat16),
        compiler_params=KERNEL_PARAMS,
        cost_estimate=pl.CostEstimate(
            flops=pairs * 14 * LEN * LEN * PAIR,
            bytes_accessed=pairs * LEN * PAIR * 16,
            transcendentals=pairs * LEN * LEN,
        ),
        name="attend_backward",
    )(core, qkv, attended, logs, out_grad)


def sum_over_dp(rows, bits):
    place = lax.axis_index("dp")
    size = lax.axis_size("dp")

    def along(value, bit):
        return lax.ppermute(value, "dp", [(i, i ^ (1 << bit)) for i in range(size)])

    for bit in bits:
        extent = rows.shape[0] // 2
        upper = (place >> bit) & 1
        kept = lax.dynamic_slice_in_dim(rows, upper * extent, extent, 0)
        sent = lax.dynamic_slice_in_dim(rows, (1 - upper) * extent, extent, 0)
        rows = (kept.astype(jnp.float32) + along(sent, bit).astype(jnp.float32)).astype(
            jnp.bfloat16
        )
    for bit in reversed(bits):
        other = along(rows, bit)
        rows = jnp.where(
            ((place >> bit) & 1) == 0,
            jnp.concatenate([rows, other], axis=0),
            jnp.concatenate([other, rows], axis=0),
        )
    return rows


def local(
    tokens,
    ln1_gain,
    ln1_shift,
    qkv_weight,
    qv_bias,
    out_weight,
    out_bias,
    ln2_gain,
    ln2_shift,
    fc_weight,
    fc_bias,
    proj_weight,
    proj_bias,
    cotangent,
):
    size = lax.axis_size("tensor")
    place = lax.axis_index("tensor")
    near = [(i, i ^ 1) for i in range(size)]
    far = [(i, (i + size // 2) % size) for i in range(size)]
    core = (place % 2).astype(jnp.int32).reshape(1)
    own_rows, d = tokens.shape
    width = qkv_weight.shape[2]
    hidden_width = fc_weight.shape[1]
    assert size == 4 and 2 * own_rows == LEN

    def from_near(value):
        return lax.ppermute(value, "tensor", near)

    def from_far(value):
        return lax.ppermute(value, "tensor", far)

    biases = jnp.concatenate([qv_bias.reshape(-1), fc_bias])
    far_biases = from_far(biases)
    side = lax.axis_index("dp") % 2
    beside = [(i, i ^ 1) for i in range(lax.axis_size("dp"))]

    def from_beside(value):
        return lax.ppermute(value, "dp", beside)

    def ordered(got, handed, axis):
        return jnp.where(
            side == 0,
            jnp.concatenate([got, handed], axis=axis),
            jnp.concatenate([handed, got], axis=axis),
        )

    def half_of(value, axis):
        extent = value.shape[axis] // 2
        return lax.dynamic_slice_in_dim(value, side * extent, extent, axis)

    qkv_half, far_biases = lax.optimization_barrier((half_of(qkv_weight, 1), far_biases))
    got_qkv = from_far(qkv_half)
    got_out = from_far(half_of(out_weight, 0))
    got_fc = from_far(half_of(fc_weight, 0))
    got_proj = from_far(half_of(proj_weight, 0))
    far_qkv = ordered(got_qkv, from_beside(got_qkv), 1)
    near_cotangent = from_near(cotangent)

    tok_rows = tokens.astype(jnp.float32)
    normed1, scale1 = normalize(tok_rows)
    first_own = (normed1 * ln1_gain + ln1_shift).astype(jnp.bfloat16)
    first = jnp.concatenate([first_own, from_near(first_own)], axis=0)
    first, got_fc = lax.optimization_barrier((first, got_fc))

    pairs = 2 * width // PAIR
    qkv_both = jnp.concatenate([qkv_weight, far_qkv], axis=2)
    qkv_flat = qkv_both.reshape(3, d, pairs, PAIR).transpose(1, 2, 0, 3).reshape(d, -1)
    far_qv = far_biases[: 2 * width].reshape(2, width)
    qv_both = jnp.concatenate([qv_bias, far_qv], axis=1).reshape(2, pairs, PAIR)
    qkv_shift = jnp.stack([qv_both[0], jnp.zeros_like(qv_both[0]), qv_both[1]], axis=1).reshape(-1)
    qkv = (dot32(first, qkv_flat) + qkv_shift).astype(jnp.bfloat16)
    handed_fc = from_beside(got_fc)
    attended, logs = attend_forward(core, qkv)
    attended, handed_fc, got_proj = lax.optimization_barrier((attended, handed_fc, got_proj))
    far_out = ordered(got_out, from_beside(got_out), 0)
    far_fc = ordered(got_fc, handed_fc, 0)
    handed_proj = from_beside(got_proj)

    out_both = jnp.concatenate([out_weight, far_out], axis=0)
    branch_far = from_near(dot32(attended[own_rows:], out_both).astype(jnp.bfloat16))
    branch = dot32(attended[:own_rows], out_both) + branch_far.astype(jnp.float32)
    resid = tok_rows + branch + out_bias
    normed2, scale2 = normalize(resid)
    second_own = (normed2 * ln2_gain + ln2_shift).astype(jnp.bfloat16)
    second = jnp.concatenate([second_own, from_near(second_own)], axis=0)

    fc_both = jnp.concatenate([fc_weight, far_fc], axis=1)
    fc_shift = jnp.concatenate([fc_bias, far_biases[2 * width :]])
    hidden = dot32(second, fc_both) + fc_shift
    hidden, got_proj, handed_proj = lax.optimization_barrier((hidden, got_proj, handed_proj))
    proj_both = jnp.concatenate([proj_weight, ordered(got_proj, handed_proj, 0)], axis=0)
    active, gelu_back = jax.vjp(partial(jax.nn.gelu, approximate=True), hidden)
    active_low = active.astype(jnp.bfloat16)
    mlp_far = from_near(dot32(active_low[own_rows:], proj_both).astype(jnp.bfloat16))
    mlp_out = dot32(active_low[:own_rows], proj_both) + mlp_far.astype(jnp.float32)
    output = (resid + mlp_out + proj_bias).astype(jnp.bfloat16)

    grad_rows = cotangent.astype(jnp.float32)
    proj_bias_grad = jnp.sum(grad_rows, axis=0)
    grad_full = jnp.concatenate([cotangent, near_cotangent], axis=0)
    active_grad = dot32(grad_full, proj_both, ROWS_ROWS)
    hidden_low = gelu_back(active_grad)[0].astype(jnp.bfloat16)
    second_far = from_near(
        dot32(hidden_low[own_rows:], fc_both, ROWS_ROWS).astype(jnp.bfloat16)
    )
    second_grad = dot32(hidden_low[:own_rows], fc_both, ROWS_ROWS) + second_far.astype(jnp.float32)

    columns_columns = (((0,), (0,)), ((), ()))

    def joined(own, other):
        return (own + other.astype(jnp.float32)).astype(jnp.bfloat16)

    proj_far = from_far(
        dot32(active_low[:, hidden_width:], grad_full, columns_columns).astype(jnp.bfloat16)
    )
    proj_own = dot32(active_low[:, :hidden_width], grad_full, columns_columns)
    fc_far = from_far(
        dot32(second, hidden_low[:, hidden_width:], columns_columns).astype(jnp.bfloat16)
    )
    fc_own = dot32(second, hidden_low[:, :hidden_width], columns_columns)
    fc_sums = jnp.sum(hidden_low, axis=0, dtype=jnp.float32)

    resid_grad = grad_rows + norm_back(second_grad, normed2, scale2, ln2_gain)
    branch_low = resid_grad.astype(jnp.bfloat16)
    branch_full = jnp.concatenate([branch_low, from_near(branch_low)], axis=0)
    ln2_gain_grad = jnp.sum(second_grad * normed2, axis=0)
    ln2_shift_grad = jnp.sum(second_grad, axis=0)
    out_bias_grad = jnp.sum(branch_low, axis=0, dtype=jnp.float32)
    heads_grad = dot32(branch_full, out_both, ROWS_ROWS).astype(jnp.bfloat16)
    out_both_grad = dot32(attended, branch_full, columns_columns)

    qkv_grad = attend_backward(core, qkv, attended, logs, heads_grad)
    fc_own, proj_own, late_grad = lax.optimization_barrier((fc_own, proj_own, qkv_grad))
    bits = range(lax.axis_size("dp").bit_length() - 1)
    fc_weight_grad = sum_over_dp(joined(fc_own, fc_far), [*bits]).astype(jnp.float32)
    proj_weight_grad = sum_over_dp(joined(proj_own, proj_far), [*bits][1:] + [0]).astype(
        jnp.float32
    )
    qkv_sums = jnp.sum(late_grad, axis=0, dtype=jnp.float32).reshape(pairs, 3, PAIR)
    qv_sums = qkv_sums[:, 0::2].transpose(1, 0, 2).reshape(2, 2 * width)
    qkv_both_grad = dot32(qkv_grad, first, columns_columns).reshape(pairs, 3, PAIR, d)
    qkv_both_grad = qkv_both_grad.transpose(1, 0, 2, 3).reshape(3, 2, width, d)
    last_far = from_far(
        jnp.concatenate(
            [qkv_both_grad[:, 1].reshape(3 * width, d), out_both_grad[width:]], axis=0
        ).astype(jnp.bfloat16)
    )
    last_own = jnp.concatenate(
        [qkv_both_grad[:, 0].reshape(3 * width, d), out_both_grad[:width]], axis=0
    )

    first_far = from_near(dot32(qkv_grad[own_rows:], qkv_flat, ROWS_ROWS).astype(jnp.bfloat16))
    first_grad = dot32(qkv_grad[:own_rows], qkv_flat, ROWS_ROWS) + first_far.astype(jnp.float32)
    ln1_gain_grad = jnp.sum(first_grad * normed1, axis=0)
    ln1_shift_grad = jnp.sum(first_grad, axis=0)
    tokens_grad = resid_grad + norm_back(first_grad, normed1, scale1, ln1_gain)

    gains = jnp.concatenate(
        [
            ln1_gain_grad,
            ln1_shift_grad,
            out_bias_grad,
            ln2_gain_grad,
            ln2_shift_grad,
            proj_bias_grad,
        ]
    )
    gains = gains + from_near(gains)
    split = qv_sums.reshape(2, 2, width)
    split_far = from_far(
        jnp.concatenate([gains, split[:, 1].reshape(-1), fc_sums[hidden_width:]])
    )
    split_own = jnp.concatenate([gains, split[:, 0].reshape(-1), fc_sums[:hidden_width]])
    small_part = split_own + split_far
    edge = 4 * width
    cut = edge * 2 // 3
    short = -small_part.shape[0] % d
    small_part = jnp.pad(small_part, (0, short)).reshape(-1, d)
    small_rows = -(-small_part.shape[0] // 128) * 128
    small_part = jnp.pad(small_part, ((0, small_rows - small_part.shape[0]), (0, 0)))
    last_low = joined(last_own, last_far)
    early = last_low[:cut]
    late = jnp.concatenate([last_low[cut:], small_part.astype(jnp.bfloat16)], axis=0)
    early = sum_over_dp(early, [*bits])
    late = sum_over_dp(late, [*bits][1:] + [0])
    qkv_low = jnp.concatenate([early, late], axis=0)[: 3 * width].reshape(3, width, d)
    qkv_weight_grad = qkv_low.astype(jnp.float32).transpose(0, 2, 1)
    out_weight_grad = late[3 * width - cut : edge - cut].astype(jnp.float32)
    small = late[edge - cut :].astype(jnp.float32).reshape(-1)
    ln1_gain_grad, ln1_shift_grad, out_bias_grad, ln2_gain_grad, ln2_shift_grad, proj_bias_grad = (
        small[at * d : (at + 1) * d] for at in range(6)
    )
    qv_bias_grad = small[6 * d : 6 * d + 2 * width].reshape(2, width)
    fc_bias_grad = small[6 * d + 2 * width : 6 * d + 2 * width + hidden_width]
    return (
        output,
        tokens_grad,
        ln1_gain_grad,
        ln1_shift_grad,
        qkv_weight_grad,
        qv_bias_grad,
        out_weight_grad,
        out_bias_grad,
        ln2_gain_grad,
        ln2_shift_grad,
        fc_weight_grad,
        fc_bias_grad,
        proj_weight_grad,
        proj_bias_grad,
    )


def solution(mesh):
    return jax.shard_map(
        local,
        mesh=mesh,
        in_specs=(
            P(("dp", "tensor"), None),
            P(),
            P(),
            P(None, None, "tensor"),
            P(None, "tensor"),
            P("tensor", None),
            P(),
            P(),
            P(),
            P(None, "tensor"),
            P("tensor"),
            P("tensor", None),
            P(),
            P(("dp", "tensor"), None),
        ),
        out_specs=(
            P(("dp", "tensor"), None),
            P(("dp", "tensor"), None),
            P(),
            P(),
            P(None, None, "tensor"),
            P(None, "tensor"),
            P("tensor", None),
            P(),
            P(),
            P(),
            P(None, "tensor"),
            P("tensor"),
            P("tensor", None),
            P(),
        ),
        check_vma=False,
    )
```

```python
from functools import partial

import jax
import jax.numpy as jnp
from jax import lax
from jax.experimental import pallas as pl
from jax.experimental.pallas import tpu as pltpu
from jax.sharding import PartitionSpec as P

HEAD_DIM = 64
PAIR = 2 * HEAD_DIM
LEN = 1024
BLOCK = 256
NORM_EPSILON = 1e-05
SCORE_SCALE = 1.4426950408889634 * HEAD_DIM**-0.5

ROWS_ROWS = (((1,), (1,)), ((), ()))


def normalize(values):
    row_mean = jnp.mean(values, axis=-1, keepdims=True)
    centred = values - row_mean
    variance = jnp.mean(centred * centred, axis=-1, keepdims=True)
    row_scale = lax.rsqrt(variance + NORM_EPSILON)
    return (centred * row_scale, row_scale)


def norm_back(grad_in, normed, row_scale, gain_vec):
    shaped = grad_in * gain_vec
    return row_scale * (
        shaped
        - jnp.mean(shaped, axis=-1, keepdims=True)
        - normed * jnp.mean(shaped * normed, axis=-1, keepdims=True)
    )


def dot32(left, right, dims=(((1,), (0,)), ((), ()))):
    return lax.dot_general(left, right, dims, preferred_element_type=jnp.float32)


def half_starts(core_ref):
    half = LEN // 2
    first = pl.multiple_of(core_ref[0] * half, half)
    second = pl.multiple_of(half - core_ref[0] * half, half)
    return first, second


def in_order(ref, starts):
    half = LEN // 2
    return jnp.concatenate([ref[pl.ds(start, half), :] for start in starts], axis=0)


def block_rows(starts, step):
    half = LEN // 2
    offset = step * BLOCK
    start = starts[offset // half] + offset % half
    return pl.ds(pl.multiple_of(start, BLOCK), BLOCK)


def split_heads(block):
    low_lanes = lax.broadcasted_iota(jnp.int32, block.shape, 1) < HEAD_DIM
    zero = jnp.zeros_like(block)
    return jnp.concatenate(
        [jnp.where(low_lanes, block, zero), jnp.where(low_lanes, zero, block)], axis=0
    )


def causal_keep():
    keys = lax.broadcasted_iota(jnp.int32, (BLOCK, 2 * BLOCK), 0)
    queries = lax.broadcasted_iota(jnp.int32, (BLOCK, 2 * BLOCK), 1) % BLOCK
    return keys <= queries


def attend_forward_kernel(core_ref, qkv_ref, out_ref, log_ref):
    starts = half_starts(core_ref)
    full = in_order(qkv_ref, starts)
    keys = full[:, PAIR : 2 * PAIR]
    values_t = full[:, 2 * PAIR :].T
    keep = causal_keep()
    for step in range(LEN // BLOCK):
        seen = (step + 1) * BLOCK
        queries = split_heads(full[step * BLOCK : seen, :PAIR])
        scores = dot32(keys[:seen], queries, ROWS_ROWS)
        last = jnp.where(keep, scores[seen - BLOCK :], -1e30)
        scores = jnp.concatenate([scores[: seen - BLOCK], last], axis=0) if step else last
        top = jnp.max(scores, axis=0, keepdims=True) * SCORE_SCALE
        exponent = jnp.exp2(scores * SCORE_SCALE - top)
        total = jnp.sum(exponent, axis=0, keepdims=True)
        low = exponent.astype(jnp.bfloat16)
        inverse = 1.0 / total
        logs = top + jnp.log2(total)
        parts = []
        for head in range(2):
            columns = slice(head * BLOCK, (head + 1) * BLOCK)
            attended = dot32(
                values_t[head * HEAD_DIM : (head + 1) * HEAD_DIM, :seen], low[:, columns]
            )
            parts.append(attended * inverse[:, columns])
            log_ref[0, head : head + 1, step * BLOCK : seen] = logs[:, columns]
        out_ref[block_rows(starts, step), :] = (
            jnp.concatenate(parts, axis=0).T.astype(jnp.bfloat16)
        )


def attend_backward_kernel(core_ref, qkv_ref, out_ref, log_ref, grad_ref, dqkv_ref, dk_ref, dv_ref):
    starts = half_starts(core_ref)
    full = in_order(qkv_ref, starts)
    out_grad = in_order(grad_ref, starts)
    attended = in_order(out_ref, starts)
    keys = full[:, PAIR : 2 * PAIR]
    values = full[:, 2 * PAIR :]
    keys_t = keys.T
    product_t = (out_grad.astype(jnp.float32) * attended.astype(jnp.float32)).T
    deltas = [
        jnp.sum(product_t[head * HEAD_DIM : (head + 1) * HEAD_DIM], axis=0, keepdims=True)
        for head in range(2)
    ]
    keep = causal_keep()
    factor = HEAD_DIM**-0.5
    steps = LEN // BLOCK
    for step in reversed(range(steps)):
        seen = (step + 1) * BLOCK
        columns = slice(step * BLOCK, seen)
        queries = split_heads(full[columns, :PAIR])
        grads = split_heads(out_grad[columns])
        logs = jnp.concatenate([log_ref[0, 0:1, columns], log_ref[0, 1:2, columns]], axis=1)
        delta = jnp.concatenate([deltas[0][:, columns], deltas[1][:, columns]], axis=1)
        scores = dot32(keys[:seen], queries, ROWS_ROWS)
        weights = jnp.exp2(scores * SCORE_SCALE - logs)
        last = jnp.where(keep, weights[seen - BLOCK :], 0.0)
        weights = jnp.concatenate([weights[: seen - BLOCK], last], axis=0) if step else last
        weight_grad = dot32(values[:seen], grads, ROWS_ROWS)
        value_term = dot32(weights.astype(jnp.bfloat16), grads)
        score_grad = (weights * (weight_grad - delta)).astype(jnp.bfloat16)
        key_term = dot32(score_grad, queries)
        if step == steps - 1:
            dk_ref[...] = key_term
            dv_ref[...] = value_term
        else:
            dk_ref[:seen, :] += key_term
            dv_ref[:seen, :] += value_term
        parts = [
            dot32(
                keys_t[head * HEAD_DIM : (head + 1) * HEAD_DIM, :seen],
                score_grad[:, head * BLOCK : (head + 1) * BLOCK],
            )
            for head in range(2)
        ]
        query_grad = jnp.concatenate(parts, axis=0).T * factor
        dqkv_ref[block_rows(starts, step), :PAIR] = query_grad.astype(jnp.bfloat16)
    half = LEN // 2
    for at, start in enumerate(starts):
        rows = slice(at * half, (at + 1) * half)
        dqkv_ref[pl.ds(start, half), PAIR : 2 * PAIR] = (dk_ref[rows, :] * factor).astype(
            jnp.bfloat16
        )
        dqkv_ref[pl.ds(start, half), 2 * PAIR :] = dv_ref[rows, :].astype(jnp.bfloat16)


def pair_block(width):
    return pl.BlockSpec((LEN, width), lambda pair, core: (0, pair))


LOG_BLOCK = pl.BlockSpec((1, 8, LEN), lambda pair, core: (pair, 0, 0))
KERNEL_PARAMS = pltpu.CompilerParams(vmem_limit_bytes=40 * 1024 * 1024)


def attend_forward(core, qkv):
    pairs = qkv.shape[1] // (3 * PAIR)
    return pl.pallas_call(
        attend_forward_kernel,
        grid_spec=pltpu.PrefetchScalarGridSpec(
            num_scalar_prefetch=1,
            grid=(pairs,),
            in_specs=[pair_block(3 * PAIR)],
            out_specs=[pair_block(PAIR), LOG_BLOCK],
        ),
        out_shape=[
            jax.ShapeDtypeStruct((LEN, pairs * PAIR), jnp.bfloat16),
            jax.ShapeDtypeStruct((pairs, 8, LEN), jnp.float32),
        ],
        compiler_params=KERNEL_PARAMS,
        cost_estimate=pl.CostEstimate(
            flops=pairs * 5 * LEN * LEN * PAIR,
            bytes_accessed=pairs * LEN * PAIR * 8,
            transcendentals=pairs * LEN * LEN,
        ),
        name="attend_forward",
    )(core, qkv)


def attend_backward(core, qkv, attended, logs, out_grad):
    pairs = qkv.shape[1] // (3 * PAIR)
    return pl.pallas_call(
        attend_backward_kernel,
        grid_spec=pltpu.PrefetchScalarGridSpec(
            num_scalar_prefetch=1,
            grid=(pairs,),
            in_specs=[pair_block(3 * PAIR), pair_block(PAIR), LOG_BLOCK, pair_block(PAIR)],
            out_specs=pair_block(3 * PAIR),
            scratch_shapes=[
                pltpu.VMEM((LEN, PAIR), jnp.float32),
                pltpu.VMEM((LEN, PAIR), jnp.float32),
            ],
        ),
        out_shape=jax.ShapeDtypeStruct(qkv.shape, jnp.bfloat16),
        compiler_params=KERNEL_PARAMS,
        cost_estimate=pl.CostEstimate(
            flops=pairs * 14 * LEN * LEN * PAIR,
            bytes_accessed=pairs * LEN * PAIR * 16,
            transcendentals=pairs * LEN * LEN,
        ),
        name="attend_backward",
    )(core, qkv, attended, logs, out_grad)


def halves(rows, upper):
    extent = rows.shape[-2] // 2
    axis = rows.ndim - 2
    kept = lax.dynamic_slice_in_dim(rows, upper * extent, extent, axis)
    sent = lax.dynamic_slice_in_dim(rows, (1 - upper) * extent, extent, axis)
    return kept, sent


def joined(own, other):
    return (own.astype(jnp.float32) + other.astype(jnp.float32)).astype(jnp.bfloat16)


def sum_over_dp(rows, bits, far=None):
    place = lax.axis_index("dp")
    size = lax.axis_size("dp")

    def along(value, bit):
        return lax.ppermute(value, "dp", [(i, i ^ (1 << bit)) for i in range(size)])

    for step, bit in enumerate(bits):
        upper = (place >> bit) & 1
        if step == 0 and far is not None:
            kept, sent = halves(far, upper)
            far = joined(kept, along(sent, bit))
            kept, sent = halves(rows, upper)
            rows = joined(kept, along(sent, bit))
            size_t = lax.axis_size("tensor")
            across = [(i, (i + size_t // 2) % size_t) for i in range(size_t)]
            rows = joined(rows, lax.ppermute(far, "tensor", across))
        else:
            kept, sent = halves(rows, upper)
            rows = joined(kept, along(sent, bit))
    for bit in reversed(bits):
        other = along(rows, bit)
        rows = jnp.where(
            ((place >> bit) & 1) == 0,
            jnp.concatenate([rows, other], axis=0),
            jnp.concatenate([other, rows], axis=0),
        )
    return rows


def local(
    tokens,
    ln1_gain,
    ln1_shift,
    qkv_weight,
    qv_bias,
    out_weight,
    out_bias,
    ln2_gain,
    ln2_shift,
    fc_weight,
    fc_bias,
    proj_weight,
    proj_bias,
    cotangent,
):
    size = lax.axis_size("tensor")
    place = lax.axis_index("tensor")
    near = [(i, i ^ 1) for i in range(size)]
    far = [(i, (i + size // 2) % size) for i in range(size)]
    core = (place % 2).astype(jnp.int32).reshape(1)
    own_rows, d = tokens.shape
    width = qkv_weight.shape[2]
    hidden_width = fc_weight.shape[1]
    assert size == 4 and 2 * own_rows == LEN

    def from_near(value):
        return lax.ppermute(value, "tensor", near)

    def from_far(value):
        return lax.ppermute(value, "tensor", far)

    biases = jnp.concatenate([qv_bias.reshape(-1), fc_bias])
    far_biases = from_far(biases)
    side = lax.axis_index("dp") % 2
    beside = [(i, i ^ 1) for i in range(lax.axis_size("dp"))]

    def from_beside(value):
        return lax.ppermute(value, "dp", beside)

    def ordered(got, handed, axis):
        return jnp.where(
            side == 0,
            jnp.concatenate([got, handed], axis=axis),
            jnp.concatenate([handed, got], axis=axis),
        )

    def half_of(value, axis):
        extent = value.shape[axis] // 2
        return lax.dynamic_slice_in_dim(value, side * extent, extent, axis)

    qkv_half, far_biases = lax.optimization_barrier((half_of(qkv_weight, 1), far_biases))
    got_qkv = from_far(qkv_half)
    got_out = from_far(half_of(out_weight, 0))
    got_fc = from_far(half_of(fc_weight, 0))
    got_proj = from_far(half_of(proj_weight, 0))
    far_qkv = ordered(got_qkv, from_beside(got_qkv), 1)
    near_cotangent = from_near(cotangent)

    tok_rows = tokens.astype(jnp.float32)
    normed1, scale1 = normalize(tok_rows)
    first_own = (normed1 * ln1_gain + ln1_shift).astype(jnp.bfloat16)
    first = jnp.concatenate([first_own, from_near(first_own)], axis=0)
    first, got_fc = lax.optimization_barrier((first, got_fc))

    pairs = 2 * width // PAIR
    qkv_both = jnp.concatenate([qkv_weight, far_qkv], axis=2)
    qkv_flat = qkv_both.reshape(3, d, pairs, PAIR).transpose(1, 2, 0, 3).reshape(d, -1)
    far_qv = far_biases[: 2 * width].reshape(2, width)
    qv_both = jnp.concatenate([qv_bias, far_qv], axis=1).reshape(2, pairs, PAIR)
    qkv_shift = jnp.stack([qv_both[0], jnp.zeros_like(qv_both[0]), qv_both[1]], axis=1).reshape(-1)
    qkv = (dot32(first, qkv_flat) + qkv_shift).astype(jnp.bfloat16)
    handed_fc = from_beside(got_fc)
    attended, logs = attend_forward(core, qkv)
    attended, handed_fc, got_proj = lax.optimization_barrier((attended, handed_fc, got_proj))
    far_out = ordered(got_out, from_beside(got_out), 0)
    far_fc = ordered(got_fc, handed_fc, 0)
    handed_proj = from_beside(got_proj)

    out_both = jnp.concatenate([out_weight, far_out], axis=0)
    branch_far = from_near(dot32(attended[own_rows:], out_both).astype(jnp.bfloat16))
    branch = dot32(attended[:own_rows], out_both) + branch_far.astype(jnp.float32)
    resid = tok_rows + branch + out_bias
    normed2, scale2 = normalize(resid)
    second_own = (normed2 * ln2_gain + ln2_shift).astype(jnp.bfloat16)
    second = jnp.concatenate([second_own, from_near(second_own)], axis=0)

    fc_both = jnp.concatenate([fc_weight, far_fc], axis=1)
    fc_shift = jnp.concatenate([fc_bias, far_biases[2 * width :]])
    hidden = dot32(second, fc_both) + fc_shift
    hidden, got_proj, handed_proj = lax.optimization_barrier((hidden, got_proj, handed_proj))
    proj_both = jnp.concatenate([proj_weight, ordered(got_proj, handed_proj, 0)], axis=0)
    active, gelu_back = jax.vjp(partial(jax.nn.gelu, approximate=True), hidden)
    active_low = active.astype(jnp.bfloat16)
    mlp_far = from_near(dot32(active_low[own_rows:], proj_both).astype(jnp.bfloat16))
    mlp_out = dot32(active_low[:own_rows], proj_both) + mlp_far.astype(jnp.float32)
    output = (resid + mlp_out + proj_bias).astype(jnp.bfloat16)

    grad_rows = cotangent.astype(jnp.float32)
    proj_bias_grad = jnp.sum(grad_rows, axis=0)
    grad_full = jnp.concatenate([cotangent, near_cotangent], axis=0)
    active_grad = dot32(grad_full, proj_both, ROWS_ROWS)
    hidden_low = gelu_back(active_grad)[0].astype(jnp.bfloat16)
    second_far = from_near(
        dot32(hidden_low[own_rows:], fc_both, ROWS_ROWS).astype(jnp.bfloat16)
    )
    second_grad = dot32(hidden_low[:own_rows], fc_both, ROWS_ROWS) + second_far.astype(jnp.float32)

    columns_columns = (((0,), (0,)), ((), ()))

    proj_far = from_far(
        dot32(active_low[:, hidden_width:], grad_full, columns_columns).astype(jnp.bfloat16)
    )
    proj_own = dot32(active_low[:, :hidden_width], grad_full, columns_columns)
    fc_other = dot32(second, hidden_low[:, hidden_width:], columns_columns).astype(jnp.bfloat16)
    fc_own = dot32(second, hidden_low[:, :hidden_width], columns_columns).astype(jnp.bfloat16)
    fc_sums = jnp.sum(hidden_low, axis=0, dtype=jnp.float32)

    resid_grad = grad_rows + norm_back(second_grad, normed2, scale2, ln2_gain)
    branch_low = resid_grad.astype(jnp.bfloat16)
    branch_full = jnp.concatenate([branch_low, from_near(branch_low)], axis=0)
    ln2_gain_grad = jnp.sum(second_grad * normed2, axis=0)
    ln2_shift_grad = jnp.sum(second_grad, axis=0)
    out_bias_grad = jnp.sum(branch_low, axis=0, dtype=jnp.float32)
    heads_grad = dot32(branch_full, out_both, ROWS_ROWS).astype(jnp.bfloat16)
    out_both_grad = dot32(attended, branch_full, columns_columns)

    qkv_grad = attend_backward(core, qkv, attended, logs, heads_grad)
    fc_own, proj_own, late_grad = lax.optimization_barrier((fc_own, proj_own, qkv_grad))
    bits = range(lax.axis_size("dp").bit_length() - 1)
    fc_weight_grad = sum_over_dp(fc_own, [*bits], fc_other).astype(jnp.float32)
    proj_weight_grad = sum_over_dp(joined(proj_own, proj_far), [*bits][1:] + [0]).astype(
        jnp.float32
    )
    qkv_sums = jnp.sum(late_grad, axis=0, dtype=jnp.float32).reshape(pairs, 3, PAIR)
    qv_sums = qkv_sums[:, 0::2].transpose(1, 0, 2).reshape(2, 2 * width)
    qkv_both_grad = dot32(qkv_grad, first, columns_columns).reshape(pairs, 3, PAIR, d)
    qkv_both_grad = qkv_both_grad.transpose(1, 0, 2, 3).reshape(3, 2, width, d)
    last_far = from_far(
        jnp.concatenate(
            [qkv_both_grad[:, 1].reshape(3 * width, d), out_both_grad[width:]], axis=0
        ).astype(jnp.bfloat16)
    )
    last_own = jnp.concatenate(
        [qkv_both_grad[:, 0].reshape(3 * width, d), out_both_grad[:width]], axis=0
    )

    first_far = from_near(dot32(qkv_grad[own_rows:], qkv_flat, ROWS_ROWS).astype(jnp.bfloat16))
    first_grad = dot32(qkv_grad[:own_rows], qkv_flat, ROWS_ROWS) + first_far.astype(jnp.float32)
    ln1_gain_grad = jnp.sum(first_grad * normed1, axis=0)
    ln1_shift_grad = jnp.sum(first_grad, axis=0)
    tokens_grad = resid_grad + norm_back(first_grad, normed1, scale1, ln1_gain)

    gains = jnp.concatenate(
        [
            ln1_gain_grad,
            ln1_shift_grad,
            out_bias_grad,
            ln2_gain_grad,
            ln2_shift_grad,
            proj_bias_grad,
        ]
    )
    gains = gains + from_near(gains)
    split = qv_sums.reshape(2, 2, width)
    split_far = from_far(
        jnp.concatenate([gains, split[:, 1].reshape(-1), fc_sums[hidden_width:]])
    )
    split_own = jnp.concatenate([gains, split[:, 0].reshape(-1), fc_sums[:hidden_width]])
    small_part = split_own + split_far
    edge = 4 * width
    cut = edge * 2 // 3
    short = -small_part.shape[0] % d
    small_part = jnp.pad(small_part, (0, short)).reshape(-1, d)
    small_rows = -(-small_part.shape[0] // 128) * 128
    small_part = jnp.pad(small_part, ((0, small_rows - small_part.shape[0]), (0, 0)))
    last_low = joined(last_own, last_far)
    early = last_low[:cut]
    late = jnp.concatenate([last_low[cut:], small_part.astype(jnp.bfloat16)], axis=0)
    early = sum_over_dp(early, [*bits])
    late = sum_over_dp(late, [*bits][1:] + [0])
    qkv_low = jnp.concatenate([early, late], axis=0)[: 3 * width].reshape(3, width, d)
    qkv_weight_grad = qkv_low.astype(jnp.float32).transpose(0, 2, 1)
    out_weight_grad = late[3 * width - cut : edge - cut].astype(jnp.float32)
    small = late[edge - cut :].astype(jnp.float32).reshape(-1)
    ln1_gain_grad, ln1_shift_grad, out_bias_grad, ln2_gain_grad, ln2_shift_grad, proj_bias_grad = (
        small[at * d : (at + 1) * d] for at in range(6)
    )
    qv_bias_grad = small[6 * d : 6 * d + 2 * width].reshape(2, width)
    fc_bias_grad = small[6 * d + 2 * width : 6 * d + 2 * width + hidden_width]
    return (
        output,
        tokens_grad,
        ln1_gain_grad,
        ln1_shift_grad,
        qkv_weight_grad,
        qv_bias_grad,
        out_weight_grad,
        out_bias_grad,
        ln2_gain_grad,
        ln2_shift_grad,
        fc_weight_grad,
        fc_bias_grad,
        proj_weight_grad,
        proj_bias_grad,
    )


def solution(mesh):
    return jax.shard_map(
        local,
        mesh=mesh,
        in_specs=(
            P(("dp", "tensor"), None),
            P(),
            P(),
            P(None, None, "tensor"),
            P(None, "tensor"),
            P("tensor", None),
            P(),
            P(),
            P(),
            P(None, "tensor"),
            P("tensor"),
            P("tensor", None),
            P(),
            P(("dp", "tensor"), None),
        ),
        out_specs=(
            P(("dp", "tensor"), None),
            P(("dp", "tensor"), None),
            P(),
            P(),
            P(None, None, "tensor"),
            P(None, "tensor"),
            P("tensor", None),
            P(),
            P(),
            P(),
            P(None, "tensor"),
            P("tensor"),
            P("tensor", None),
            P(),
        ),
        check_vma=False,
    )
```
